32 devices in a mesh: ctx: 16 (over z, y, core), head: 2 (over x).
Axes of the slice: x: 2, y: 2, z: 4, core: 2. Of those that a mesh axis runs over, the one named last changes fastest.
Arguments:
- query_rows: bfloat16 [8192, 1536], P(('ctx', 'head')), may hold values from -51 to 51
- key_rows: bfloat16 [8192, 1536], P(('ctx', 'head')), may hold values from -6 to 6
- value_rows: bfloat16 [8192, 1536], P(('ctx', 'head')), may hold values from -12 to 12
- residual: bfloat16 [8192, 1536], P(('ctx', 'head')), may hold values from -6 to 6
- levels: int32 [16], P('ctx'), may hold values from 0 to 49
- gate_table: float32 [50, 1536], replicated, may hold values from -4 to 4
- block_mask: int32 [16, 7, 4, 4], P('ctx'), may hold values from 0 to 1, as said below
- out_weight: bfloat16 [1536, 1536], P('head'), may hold values from -0.15625 to 0.15625
Outputs:
- mixed: bfloat16 [8192, 1536], P(('ctx', 'head'))
The draws below stay inside these ranges and needn't reach their ends.
Inputs may be any that keep to these rules, and one draw needn't show every extreme that they name: block_mask[f, s, a, b] = 1 lets query block a of frame f attend key block b of frame f + offset(s); slot 0 is all ones; entries whose frame f + offset(s) lies outside the clip are 0.
All inputs are finite; a program needn't handle non-finite values.
Results may differ from the reference program's by a relative error of at most 0.0065.
Values may be sent and summed in bfloat16 or wider, within the bound.
A program may use at most 64 MiB of HBM per device.

```python
import math
import jax
import jax.numpy as jnp
from jax import lax

D = 1536
HEADS = 12
HEAD_DIM = 128
FRAME = 512
BLOCK = 128
LOGR = 3
LEVELS = 50
SLOTS = 7
FRAMES = 16
TOKENS = 8192
BLOCKS = 4


def drawn_pair(key):
    key_first = jax.random.fold_in(key, 11)
    key_second = jax.random.fold_in(key, 23)
    keys_base = jnp.clip(jax.random.normal(key_first, (TOKENS, D), jnp.float32), -6.0, 6.0)
    queries = jnp.clip(1.5 * jax.random.normal(key_second, (TOKENS, D), jnp.float32), -9.0, 9.0)
    return (queries, keys_base)


def draw_query_rows(key, part):
    return drawn_pair(key)[0].astype(jnp.bfloat16)


def draw_key_rows(key, part):
    return drawn_pair(key)[1].astype(jnp.bfloat16)


def draw_block_mask(key, part):
    dice_rolls = jax.random.randint(key, (FRAMES, SLOTS, BLOCKS, BLOCKS), 0, 2 ** LOGR, dtype=jnp.int32)
    slot_ids = jnp.arange(SLOTS, dtype=jnp.int32)
    octave = jnp.maximum((slot_ids - 1) // 2, 0)
    distance = jnp.left_shift(jnp.ones_like(octave), octave)
    offset_row = jnp.where(slot_ids == 0, 0, jnp.where(slot_ids % 2 == 1, -distance, distance))
    partner = jnp.arange(FRAMES, dtype=jnp.int32)[:, None] + offset_row[None, :]
    inside = (partner >= 0) & (partner < FRAMES)
    threshold = jnp.left_shift(jnp.ones_like(octave), LOGR - 1 - octave)
    kept_pairs = (dice_rolls < threshold[None, :, None, None]) & inside[:, :, None, None]
    kept_pairs = kept_pairs | (slot_ids == 0)[None, :, None, None]
    return kept_pairs.astype(jnp.int32)


def place_ends(result, stream_key, low, largest):
    extent = result.shape
    index_at = [jax.random.randint(jax.random.fold_in(stream_key, axis), (), 0, extent[axis]) for axis in range(len(extent))]
    result = result.at[tuple(index_at)].set(low)
    longest = extent.index(max(extent))
    index_at[longest] = (index_at[longest] + 1) % extent[longest]
    return result.at[tuple(index_at)].set(largest)


def steps_of(own_key, shape, pieces, smallest, largest):
    def one(dim, shards_of):
        steps = jax.random.uniform(jax.random.fold_in(jax.random.fold_in(own_key, 6), dim), (shards_of,), jnp.float32, smallest / len(pieces), largest / len(pieces))
        return jnp.repeat(jnp.exp(steps), shape[dim] // shards_of).reshape((-1,) + (1,) * (len(shape) - dim - 1))

    loudness = one(*pieces[0])
    for cut in pieces[1:]:
        loudness = loudness * one(*cut)
    return loudness


def bell_draw(stream_key, shape, width, most, split=(), held_as=jnp.bfloat16):
    array = jax.random.normal(stream_key, shape, jnp.float32) * width
    if len(split) > 0:
        array = steps_of(stream_key, shape, split, -0.22, 0.18) * array
    return jnp.clip(array, min=-most, max=most).astype(held_as)


def setup_inputs(seed: int = 0) -> dict:
    arg_keys = jax.random.split(jax.random.key(seed), 9)
    return {
        "query_rows": draw_query_rows(jax.random.fold_in(arg_keys[8], 71), 0),
        "key_rows": draw_key_rows(jax.random.fold_in(arg_keys[8], 71), 0),
        "value_rows": bell_draw(arg_keys[2], (TOKENS, D), 2.0, 12.0, ((0, 32),)),
        "residual": bell_draw(arg_keys[3], (TOKENS, D), 1.0, 6.0, ((0, 32),)),
        "levels": place_ends(jax.random.randint(arg_keys[4], (FRAMES,), 0, LEVELS), jax.random.fold_in(arg_keys[4], 1), 0, LEVELS - 1).astype(jnp.int32),
        "gate_table": bell_draw(arg_keys[5], (LEVELS, D), 1.0, 4.0, (), jnp.float32),
        "block_mask": draw_block_mask(jax.random.fold_in(arg_keys[8], 71), 0),
        "out_weight": bell_draw(arg_keys[7], (D, D), D ** -0.5, 0.15625, ((0, 2),)),
    }


def offset_list():
    found_offsets = [0]
    for octave in range(LOGR):
        found_offsets.append(-2 ** octave)
        found_offsets.append(2 ** octave)
    return found_offsets

def expand_blocks(block_rows):
    blocks = block_rows.shape[0]
    broadened = jnp.broadcast_to(block_rows[:, None, :, None], (blocks, BLOCK, blocks, BLOCK))
    return broadened.reshape(blocks * BLOCK, blocks * BLOCK) > 0

def reference(query_rows, key_rows, value_rows, residual, levels, gate_table, block_mask, out_weight):
    queries_all = query_rows.reshape(FRAMES, FRAME, HEADS, HEAD_DIM)
    keys_all = key_rows.reshape(FRAMES, FRAME, HEADS, HEAD_DIM)
    values_all = value_rows.reshape(FRAMES, FRAME, HEADS, HEAD_DIM)
    inv_root = 1.0 / math.sqrt(HEAD_DIM)

    def one_frame(frame_idx):
        query_block = queries_all[frame_idx].astype(jnp.float32)
        score_list = []
        value_list = []
        for slot_idx, shift_by in enumerate(offset_list()):
            partner = jnp.clip(frame_idx + shift_by, 0, FRAMES - 1).astype(jnp.int32)
            key_block = keys_all[partner].astype(jnp.float32)
            value_block = values_all[partner].astype(jnp.float32)
            allowed = expand_blocks(block_mask[frame_idx, slot_idx])
            scores = jnp.einsum('qhd,khd->hqk', query_block, key_block) * inv_root
            score_list.append(jnp.where(allowed[None], scores, -jnp.inf))
            value_list.append(value_block)
        scores = jnp.concatenate(score_list, axis=2)
        values = jnp.concatenate(value_list, axis=0)
        row_max = lax.optimization_barrier(jnp.max(scores, axis=2, keepdims=True))
        exp_scores = jnp.exp(scores - row_max)
        row_total = lax.optimization_barrier(jnp.sum(exp_scores, axis=2))
        weights = lax.optimization_barrier(exp_scores.astype(jnp.bfloat16)).astype(jnp.float32)
        summed = jnp.einsum('hqk,khd->qhd', weights, values)
        return (summed / jnp.transpose(row_total)[:, :, None]).astype(jnp.bfloat16)
    attention = lax.map(one_frame, jnp.arange(FRAMES, dtype=jnp.int32))
    attention = attention.reshape(TOKENS, D)
    projected = jnp.dot(attention, out_weight, preferred_element_type=jnp.float32)
    gate_rows = jnp.repeat(gate_table[levels], FRAME, axis=0)
    return (residual.astype(jnp.float32) + gate_rows * projected).astype(jnp.bfloat16)
```

```python
import functools
import math

import jax
import jax.numpy as jnp
from jax import lax
from jax.experimental import pallas as pl
from jax.experimental.pallas import tpu as pltpu
from jax.sharding import PartitionSpec as P

HEAD_DIM = 128
BLOCK = 128
OFFSETS = (0, -1, 1, -2, 2, -4, 4)
MESH = pl.DeviceIdType.MESH
MASKED = -1e30
EXP_SCALE = math.log2(math.e) / math.sqrt(HEAD_DIM)


def kernel(
    n, groups, q_any, k_any, v_any, res_any, levels, gate_any, mask, w_any, out,
    kv, qb, s_ref, mx_ref, tot_ref, acc_ref, att, att_tx, w, res, gate, bias,
    loc, a2a_tx, a2a_rx, tx, rx, w_tx, w_rx, w_stx, w_srx, att_ts, att_rs, misc,
):
    f = lax.axis_index("ctx")
    x = lax.axis_index("head")
    core = lax.rem(f, 2)
    y = lax.rem(f // 2, 2)
    rows = q_any.shape[0]
    heads = kv.shape[1]
    slots = kv.shape[0]
    frame = kv.shape[3]
    blocks = frame // BLOCK
    depth = w_any.shape[0]
    half = depth // 2
    piece = half // heads
    sib = f + 1 - 2 * core
    pair = f + 2 - 4 * y
    far = f + 4 - 8 * y
    has_up = f + 4 < n
    has_down = f >= 4
    relays = jnp.logical_or(jnp.logical_and(y == 0, has_up), jnp.logical_and(y == 1, has_down))
    passes_on = jnp.logical_or(
        jnp.logical_and(core == 1, f >= 2), jnp.logical_and(core == 0, f + 2 < n)
    )

    def valid(s):
        return jnp.logical_and(f + OFFSETS[s] >= 0, f + OFFSETS[s] < n)

    def peer(j):
        return lax.rem(x + j, groups)

    def source(j):
        return lax.rem(x + groups - j, groups)

    def remote(src, dst, send, recv, dev):
        return pltpu.make_async_remote_copy(
            src_ref=src, dst_ref=dst, send_sem=send, recv_sem=recv,
            device_id=dev, device_id_type=MESH,
        )

    def cols(group, h):
        return pl.ds(pl.multiple_of((group * heads + h) * HEAD_DIM, HEAD_DIM), HEAD_DIM)

    def own_rows(group):
        return pl.ds(pl.multiple_of(group * rows, rows), rows)

    operands = (k_any, v_any, q_any)

    def landing(kind, h, group):
        if kind == 2:
            return qb.at[h, own_rows(group), :]
        return kv.at[0, h, kind, own_rows(group), :]

    def local_in(kind, h):
        return pltpu.make_async_copy(
            operands[kind].at[:, cols(x, h)], landing(kind, h, x), loc.at[kind, h]
        )

    def swap(kind, h, j, group):
        return remote(
            operands[kind].at[:, cols(peer(j), h)], landing(kind, h, group),
            a2a_tx.at[j - 1, kind, h], a2a_rx.at[j - 1, kind, h], (f, peer(j)),
        )

    def direct(which, kind, h):
        slot, dev = ((5, f + 4), (6, f - 4), (3 + y, pair), (1 + core, sib))[which]
        return remote(
            kv.at[0, h, kind], kv.at[slot, h, kind],
            tx.at[which, kind, h], rx.at[slot, kind, h], (dev, x),
        )

    def relay(kind, h):
        if kind == 0:
            src, slot, dev = 4 - y, 3 + y, far
        else:
            src, slot, dev = 6 - y, 4 - y, pair
        return remote(
            kv.at[src, h, kind], kv.at[slot, h, kind],
            tx.at[4, kind, h], rx.at[slot, kind, h], (dev, x),
        )

    def pass_on(kind, h):
        return remote(
            kv.at[4 - core, h, kind], kv.at[2 - core, h, kind],
            tx.at[5, kind, h], rx.at[2 - core, kind, h], (sib, x),
        )

    def wait_slot(slot, kind, h):
        remote(
            kv.at[0, h, kind], kv.at[slot, h, kind],
            tx.at[0, kind, h], rx.at[slot, kind, h], (sib, x),
        ).wait_recv()

    def weight_rows(group, c, t):
        return pl.ds(pl.multiple_of(group * depth + c * half + t * piece, piece), piece)

    def weight_send(t, j, group):
        return remote(
            w_any.at[pl.ds(pl.multiple_of(core * half + t * piece, piece), piece), :],
            w.at[weight_rows(group, core, t), :],
            w_tx.at[j - 1, t], w_rx.at[j - 1, t], (f, peer(j)),
        )

    def weight_share(t, j, c):
        return remote(
            w.at[weight_rows(source(j), core, t), :], w.at[weight_rows(source(j), c, t), :],
            w_stx.at[j - 1, t], w_srx.at[j - 1, t], (sib, x),
        )

    def att_send(h, j, group):
        return remote(
            att_tx.at[j - 1, h], att.at[:, cols(group, h)],
            att_ts.at[j - 1, h], att_rs.at[j - 1, h], (f, peer(j)),
        )

    others = (
        pltpu.make_async_copy(res_any, res, misc.at[0]),
        pltpu.make_async_copy(gate_any, gate, misc.at[1]),
        pltpu.make_async_copy(
            w_any, w.at[pl.ds(pl.multiple_of(x * depth, depth), depth), :], misc.at[2]
        ),
    )

    barrier = pltpu.get_barrier_semaphore()

    def greet(dev):
        pl.semaphore_signal(barrier, inc=1, device_id=dev, device_id_type=MESH)

    greet((sib, x))
    greet((pair, x))
    for j in range(1, groups):
        greet((f, peer(j)))
    pl.when(has_up)(lambda: greet((f + 4, x)))
    pl.when(has_down)(lambda: greet((f - 4, x)))

    @pl.loop(0, heads)
    def _(h):
        for kind in range(3):
            local_in(kind, h).start()

    pl.semaphore_wait(barrier, 1 + groups + has_up.astype(jnp.int32) + has_down.astype(jnp.int32))

    @pl.loop(0, heads)
    def _(h):
        for j in range(1, groups):
            for kind in range(3):
                swap(kind, h, j, x).start()

    for copy in others:
        copy.start()

    for s in range(slots):
        for a in range(blocks):
            for b in range(blocks):
                kept = mask[0, s, a, b] > 0
                bias[s, a : a + 1, b * BLOCK : (b + 1) * BLOCK] = jnp.full(
                    (1, BLOCK), jnp.where(kept, 0.0, MASKED), jnp.float32
                )

    for s in range(1, slots):

        @pl.when(jnp.logical_not(valid(s)))
        def _():
            @pl.loop(0, heads)
            def _(h):
                for kind in range(2):
                    kv[s, h, kind] = jnp.zeros((frame, HEAD_DIM), kv.dtype)

    def send_direct(h):
        for kind in range(2):
            local_in(kind, h).wait()
            for j in range(1, groups):
                swap(kind, h, j, source(j)).wait_recv()

        @pl.when(has_up)
        def _():
            for kind in range(2):
                direct(0, kind, h).start()

        @pl.when(has_down)
        def _():
            for kind in range(2):
                direct(1, kind, h).start()

        for which in (2, 3):
            for kind in range(2):
                direct(which, kind, h).start()

    def send_relay(h):
        @pl.when(relays)
        def _():
            wait_slot(4 - y, 0, h)
            relay(0, h).start()
            wait_slot(6 - y, 1, h)
            relay(1, h).start()

    def send_on(h):
        @pl.when(passes_on)
        def _():
            pl.when(jnp.logical_not(jnp.logical_and(relays, core == y)))(
                lambda: wait_slot(4 - core, 0, h)
            )
            pass_on(0, h).start()
            wait_slot(4 - core, 1, h)
            pass_on(1, h).start()

    def attend(h):
        local_in(2, h).wait()
        for j in range(1, groups):
            swap(2, h, j, source(j)).wait_recv()
        for s in range(1, slots):
            for kind in range(2):
                known = jnp.logical_and(relays, (4 - y if kind == 0 else 6 - y) == s)
                passed = jnp.logical_and(passes_on, 4 - core == s)
                due = jnp.logical_and(valid(s), jnp.logical_not(jnp.logical_or(known, passed)))
                pl.when(due)(functools.partial(wait_slot, s, kind, h))

        mx_ref[...] = jnp.full_like(mx_ref, MASKED)
        tot_ref[...] = jnp.zeros_like(tot_ref)
        acc_ref[...] = jnp.zeros_like(acc_ref)

        @pl.loop(0, slots)
        def _(s):
            for a in range(blocks):
                r = slice(a * BLOCK, (a + 1) * BLOCK)
                scores = lax.dot_general(
                    qb[h, r], kv[s, h, 0], (((1,), (1,)), ((), ())),
                    preferred_element_type=jnp.float32,
                ) + bias[s, a : a + 1, :]
                s_ref[s, r, :] = scores
                top = mx_ref[r]
                for b in range(blocks):
                    top = jnp.maximum(top, scores[:, b * BLOCK : (b + 1) * BLOCK])
                mx_ref[r] = top

        mx_ref[...] = jnp.broadcast_to(jnp.max(mx_ref[...], axis=1, keepdims=True), mx_ref.shape)

        @pl.loop(0, slots)
        def _(s):
            for a in range(blocks):
                r = slice(a * BLOCK, (a + 1) * BLOCK)
                top = mx_ref[r]
                total = tot_ref[r]
                parts = []
                for b in range(blocks):
                    e = jnp.exp2((s_ref[s, r, b * BLOCK : (b + 1) * BLOCK] - top) * EXP_SCALE)
                    total = total + e
                    parts.append(e.astype(jnp.bfloat16))
                tot_ref[r] = total
                acc_ref[r] += jnp.dot(
                    jnp.concatenate(parts, axis=1), kv[s, h, 1],
                    preferred_element_type=jnp.float32,
                )

        def share(group):
            r = own_rows(group)
            total = jnp.sum(tot_ref[r, :], axis=1, keepdims=True)
            return (acc_ref[r, :] / total).astype(jnp.bfloat16)

        for j in range(1, groups):
            att_tx[j - 1, h] = share(peer(j))
            att_send(h, j, x).start()
        att[:, cols(x, h)] = share(x)

    @pl.loop(0, heads + 3)
    def _(t):
        @pl.when(t < heads)
        def _():
            send_direct(t)
            for j in range(1, groups):
                weight_send(t, j, x).start()

        pl.when(jnp.logical_and(t >= 1, t < heads + 1))(lambda: send_relay(t - 1))
        pl.when(t >= 3)(lambda: attend(t - 3))

        @pl.when(jnp.logical_and(t >= 2, t < heads + 2))
        def _():
            send_on(t - 2)
            for j in range(1, groups):
                weight_send(t - 2, j, source(j)).wait_recv()
                weight_share(t - 2, j, core).start()

    for copy in others:
        copy.wait()

    @pl.loop(0, heads)
    def _(h):
        for j in range(1, groups):
            weight_share(h, j, 1 - core).wait_recv()
            att_send(h, j, source(j)).wait_recv()

    level = levels[0]
    gate_row = gate[pl.ds(level, 1), :]
    width = 2 * HEAD_DIM
    for at in range(0, out.shape[1], width):
        c = slice(at, at + width)
        projected = jnp.dot(att[...], w[:, c], preferred_element_type=jnp.float32)
        out[:, c] = (res[:, c].astype(jnp.float32) + gate_row[:, c] * projected).astype(out.dtype)

    @pl.loop(0, heads)
    def _(h):
        for j in range(1, groups):
            for kind in range(3):
                swap(kind, h, j, x).wait_send()
            weight_send(h, j, x).wait_send()
            weight_share(h, j, core).wait_send()
            att_send(h, j, x).wait_send()
        for kind in range(2):
            for which in (2, 3):
                direct(which, kind, h).wait_send()
            pl.when(has_up)(lambda: direct(0, kind, h).wait_send())
            pl.when(has_down)(lambda: direct(1, kind, h).wait_send())
            pl.when(relays)(lambda: relay(kind, h).wait_send())
            pl.when(passes_on)(lambda: pass_on(kind, h).wait_send())


def body(n, groups, *operands):
    query_rows, gate_table, block_mask, out_weight = (operands[i] for i in (0, 5, 6, 7))
    rows, width = query_rows.shape
    slots, blocks = block_mask.shape[1], block_mask.shape[2]
    frame = rows * groups
    heads = width // HEAD_DIM // groups
    any_space = pl.BlockSpec(memory_space=pl.ANY)
    smem = pl.BlockSpec(memory_space=pltpu.SMEM)
    bf16, f32 = jnp.bfloat16, jnp.float32
    dma = pltpu.SemaphoreType.DMA
    pairs = frame * slots * frame * heads
    return pl.pallas_call(
        functools.partial(kernel, n, groups),
        out_shape=jax.ShapeDtypeStruct((rows, width), bf16),
        in_specs=[any_space] * 4 + [smem, any_space, smem, any_space],
        out_specs=pl.BlockSpec(memory_space=pltpu.VMEM),
        scratch_shapes=[
            pltpu.VMEM((slots, heads, 2, frame, HEAD_DIM), bf16),
            pltpu.VMEM((heads, frame, HEAD_DIM), bf16),
            pltpu.VMEM((slots, frame, frame), f32),
            pltpu.VMEM((frame, HEAD_DIM), f32),
            pltpu.VMEM((frame, HEAD_DIM), f32),
            pltpu.VMEM((frame, HEAD_DIM), f32),
            pltpu.VMEM((rows, width), bf16),
            pltpu.VMEM((groups - 1, heads, rows, HEAD_DIM), bf16),
            pltpu.VMEM((width, width), bf16),
            pltpu.VMEM((rows, width), bf16),
            pltpu.VMEM(gate_table.shape, f32),
            pltpu.VMEM((slots, blocks, frame), f32),
            dma((3, heads)),
            dma((groups - 1, 3, heads)),
            dma((groups - 1, 3, heads)),
            dma((6, 2, heads)),
            dma((slots, 2, heads)),
            dma((groups - 1, heads)),
            dma((groups - 1, heads)),
            dma((groups - 1, heads)),
            dma((groups - 1, heads)),
            dma((groups - 1, heads)),
            dma((groups - 1, heads)),
            dma((3,)),
        ],
        compiler_params=pltpu.CompilerParams(
            collective_id=0, has_side_effects=True, vmem_limit_bytes=48 * 1024 * 1024
        ),
        cost_estimate=pl.CostEstimate(
            flops=4 * pairs * HEAD_DIM + 2 * rows * width * width,
            bytes_accessed=2 * (5 * rows * width + width * width // groups),
            transcendentals=pairs,
        ),
    )(*operands)


def solution(mesh):
    return jax.shard_map(
        functools.partial(body, mesh.shape["ctx"], mesh.shape["head"]),
        mesh=mesh,
        in_specs=(
            P(("ctx", "head"), None),
            P(("ctx", "head"), None),
            P(("ctx", "head"), None),
            P(("ctx", "head"), None),
            P("ctx"),
            P(),
            P("ctx", None, None, None),
            P("head", None),
        ),
        out_specs=P(("ctx", "head"), None),
        check_vma=False,
    )
```

```python
import functools
import math

import jax
import jax.numpy as jnp
from jax import lax
from jax.experimental import pallas as pl
from jax.experimental.pallas import tpu as pltpu
from jax.sharding import PartitionSpec as P

HEAD_DIM = 128
BLOCK = 128
OFFSETS = (0, -1, 1, -2, 2, -4, 4)
MESH = pl.DeviceIdType.MESH
MASKED = -1e30
AHEAD = 2
EXP_SCALE = math.log2(math.e) / math.sqrt(HEAD_DIM)


def kernel(
    n, groups, q_any, k_any, v_any, res_any, levels, gate_any, mask_any, w_any, out,
    kv, qb, s_ref, mx_ref, top_ref, tot_ref, acc_ref, att, att_tx, w, res, gate, mask, bias,
    loc, a2a_tx, a2a_rx, tx, rx, w_tx, w_rx, w_stx, w_srx, att_ts, att_rs, misc,
):
    f = lax.axis_index("ctx")
    x = lax.axis_index("head")
    core = lax.rem(f, 2)
    y = lax.rem(f // 2, 2)
    rows = q_any.shape[0]
    heads = kv.shape[1]
    slots = kv.shape[0]
    frame = kv.shape[3]
    blocks = frame // BLOCK
    depth = w_any.shape[0]
    half = depth // 2
    piece = half // heads
    sib = f + 1 - 2 * core
    pair = f + 2 - 4 * y
    far = f + 4 - 8 * y
    has_up = f + 4 < n
    has_down = f >= 4
    relays = jnp.logical_or(jnp.logical_and(y == 0, has_up), jnp.logical_and(y == 1, has_down))
    passes_on = jnp.logical_or(
        jnp.logical_and(core == 1, f >= 2), jnp.logical_and(core == 0, f + 2 < n)
    )

    def valid(s):
        return jnp.logical_and(f + OFFSETS[s] >= 0, f + OFFSETS[s] < n)

    def peer(j):
        return lax.rem(x + j, groups)

    def source(j):
        return lax.rem(x + groups - j, groups)

    def remote(src, dst, send, recv, dev):
        return pltpu.make_async_remote_copy(
            src_ref=src, dst_ref=dst, send_sem=send, recv_sem=recv,
            device_id=dev, device_id_type=MESH,
        )

    def cols(group, h):
        return pl.ds(pl.multiple_of((group * heads + h) * HEAD_DIM, HEAD_DIM), HEAD_DIM)

    def own_rows(group):
        return pl.ds(pl.multiple_of(group * rows, rows), rows)

    operands = (k_any, v_any, q_any)

    def landing(kind, h, group):
        if kind == 2:
            return qb.at[h, own_rows(group), :]
        return kv.at[0, h, kind, own_rows(group), :]

    def local_in(kind, h):
        return pltpu.make_async_copy(
            operands[kind].at[:, cols(x, h)], landing(kind, h, x), loc.at[kind, h]
        )

    def swap(kind, h, j, group):
        return remote(
            operands[kind].at[:, cols(peer(j), h)], landing(kind, h, group),
            a2a_tx.at[j - 1, kind, h], a2a_rx.at[j - 1, kind, h], (f, peer(j)),
        )

    def direct(which, kind, h):
        slot, dev = ((5, f + 4), (6, f - 4), (3 + y, pair), (1 + core, sib))[which]
        return remote(
            kv.at[0, h, kind], kv.at[slot, h, kind],
            tx.at[which, kind, h], rx.at[slot, kind, h], (dev, x),
        )

    def relay(kind, h):
        if kind == 0:
            src, slot, dev = 4 - y, 3 + y, far
        else:
            src, slot, dev = 6 - y, 4 - y, pair
        return remote(
            kv.at[src, h, kind], kv.at[slot, h, kind],
            tx.at[4, kind, h], rx.at[slot, kind, h], (dev, x),
        )

    def pass_on(kind, h):
        return remote(
            kv.at[4 - core, h, kind], kv.at[2 - core, h, kind],
            tx.at[5, kind, h], rx.at[2 - core, kind, h], (sib, x),
        )

    def wait_slot(slot, kind, h):
        remote(
            kv.at[0, h, kind], kv.at[slot, h, kind],
            tx.at[0, kind, h], rx.at[slot, kind, h], (sib, x),
        ).wait_recv()

    def weight_rows(group, c, t):
        return pl.ds(pl.multiple_of(group * depth + c * half + t * piece, piece), piece)

    def weight_send(t, j, group):
        return remote(
            w_any.at[pl.ds(pl.multiple_of(core * half + t * piece, piece), piece), :],
            w.at[weight_rows(group, core, t), :],
            w_tx.at[j - 1, t], w_rx.at[j - 1, t], (f, peer(j)),
        )

    def weight_share(t, j, c):
        return remote(
            w.at[weight_rows(source(j), core, t), :], w.at[weight_rows(source(j), c, t), :],
            w_stx.at[j - 1, t], w_srx.at[j - 1, t], (sib, x),
        )

    def att_send(h, j, group):
        return remote(
            att_tx.at[j - 1, h], att.at[:, cols(group, h)],
            att_ts.at[j - 1, h], att_rs.at[j - 1, h], (f, peer(j)),
        )

    mask_in = pltpu.make_async_copy(mask_any, mask, misc.at[3])
    mask_in.start()
    others = (
        pltpu.make_async_copy(res_any, res, misc.at[0]),
        pltpu.make_async_copy(gate_any, gate, misc.at[1]),
        pltpu.make_async_copy(
            w_any, w.at[pl.ds(pl.multiple_of(x * depth, depth), depth), :], misc.at[2]
        ),
    )

    barrier = pltpu.get_barrier_semaphore()

    def greet(dev):
        pl.semaphore_signal(barrier, inc=1, device_id=dev, device_id_type=MESH)

    greet((sib, x))
    greet((pair, x))
    for j in range(1, groups):
        greet((f, peer(j)))
    pl.when(has_up)(lambda: greet((f + 4, x)))
    pl.when(has_down)(lambda: greet((f - 4, x)))

    @pl.loop(0, heads)
    def _(h):
        for kind in range(3):
            local_in(kind, h).start()

    pl.semaphore_wait(barrier, 1 + groups + has_up.astype(jnp.int32) + has_down.astype(jnp.int32))

    def send_swap(kinds, h):
        for j in range(1, groups):
            for kind in kinds:
                swap(kind, h, j, x).start()

    for h in range(min(AHEAD, heads)):
        send_swap((0, 1), h)

    for copy in others:
        copy.start()

    mask_in.wait()
    for s in range(slots):
        off = jnp.where(mask[0, s] > 0, 0.0, MASKED)
        for b in range(blocks):
            bias[s, :, b * BLOCK : (b + 1) * BLOCK] = jnp.broadcast_to(
                off[:, b : b + 1], (blocks, BLOCK)
            )

    for s in range(1, slots):

        @pl.when(jnp.logical_not(valid(s)))
        def _():
            @pl.loop(0, heads)
            def _(h):
                for kind in range(2):
                    kv[s, h, kind] = jnp.zeros((frame, HEAD_DIM), kv.dtype)

    def send_direct(h):
        for kind in range(2):
            local_in(kind, h).wait()
            for j in range(1, groups):
                swap(kind, h, j, source(j)).wait_recv()

        @pl.when(has_up)
        def _():
            for kind in range(2):
                direct(0, kind, h).start()

        @pl.when(has_down)
        def _():
            for kind in range(2):
                direct(1, kind, h).start()

        for which in (2, 3):
            for kind in range(2):
                direct(which, kind, h).start()

    def send_relay(h):
        @pl.when(relays)
        def _():
            wait_slot(4 - y, 0, h)
            relay(0, h).start()
            wait_slot(6 - y, 1, h)
            relay(1, h).start()

    def send_on(h):
        @pl.when(passes_on)
        def _():
            for kind in range(2):
                pl.when(core != y)(functools.partial(wait_slot, 4 - core, kind, h))
                pass_on(kind, h).start()

    def early(i):
        picks = (0, 5, 6, 4 - y, 2 - core)
        slot = picks[-1]
        for k in range(len(picks) - 1):
            slot = jnp.where(i == k, picks[k], slot)
        return slot

    def late(i):
        return jnp.where(i == 0, 3 + y, 1 + core)

    def wait_slots(h, now):
        for s in range(1, slots):
            is_late = jnp.logical_or(3 + y == s, 1 + core == s)
            mine = is_late if now == "late" else jnp.logical_not(is_late)
            for kind in range(2):
                known = jnp.logical_and(relays, (4 - y if kind == 0 else 6 - y) == s)
                passed = jnp.logical_and(jnp.logical_and(passes_on, core != y), 3 + y == s)
                due = jnp.logical_and(valid(s), jnp.logical_not(jnp.logical_or(known, passed)))
                pl.when(jnp.logical_and(due, mine))(functools.partial(wait_slot, s, kind, h))

    def fold(h, count, pick, first):
        state = lax.rem(h, 2)
        if first:
            mx_ref[...] = jnp.full_like(mx_ref, MASKED)
        else:
            mx_ref[...] = top_ref[state]

        @pl.loop(0, count)
        def _(i):
            s = pick(i)
            for a in range(blocks):
                r = slice(a * BLOCK, (a + 1) * BLOCK)
                scores = lax.dot_general(
                    qb[h, r], kv[s, h, 0], (((1,), (1,)), ((), ())),
                    preferred_element_type=jnp.float32,
                ) + bias[s, a : a + 1, :]
                s_ref[i, r, :] = scores
                top = mx_ref[r]
                for b in range(blocks):
                    top = jnp.maximum(top, scores[:, b * BLOCK : (b + 1) * BLOCK])
                mx_ref[r] = top

        new_top = jnp.broadcast_to(jnp.max(mx_ref[...], axis=1, keepdims=True), mx_ref.shape)
        if first:
            tot_ref[state] = jnp.zeros(mx_ref.shape, jnp.float32)
            acc_ref[state] = jnp.zeros(mx_ref.shape, jnp.float32)
        else:
            fade = jnp.exp2((top_ref[state] - new_top) * EXP_SCALE)
            tot_ref[state] = tot_ref[state] * fade
            acc_ref[state] = acc_ref[state] * fade
        top_ref[state] = new_top

        @pl.loop(0, count)
        def _(i):
            s = pick(i)
            for a in range(blocks):
                r = slice(a * BLOCK, (a + 1) * BLOCK)
                top = top_ref[state, r]
                total = tot_ref[state, r]
                parts = []
                for b in range(blocks):
                    e = jnp.exp2((s_ref[i, r, b * BLOCK : (b + 1) * BLOCK] - top) * EXP_SCALE)
                    total = total + e
                    parts.append(e.astype(jnp.bfloat16))
                tot_ref[state, r] = total
                acc_ref[state, r] += jnp.dot(
                    jnp.concatenate(parts, axis=1), kv[s, h, 1],
                    preferred_element_type=jnp.float32,
                )

    def attend_early(h):
        local_in(2, h).wait()
        for j in range(1, groups):
            swap(2, h, j, source(j)).wait_recv()
        wait_slots(h, "early")
        fold(h, slots - 2, early, True)

    def attend_late(h):
        wait_slots(h, "late")
        fold(h, 2, late, False)
        state = lax.rem(h, 2)

        def share(group):
            r = own_rows(group)
            total = jnp.sum(tot_ref[state, r, :], axis=1, keepdims=True)
            return (acc_ref[state, r, :] / total).astype(jnp.bfloat16)

        for j in range(1, groups):
            att_tx[j - 1, h] = share(peer(j))
            att_send(h, j, x).start()
        att[:, cols(x, h)] = share(x)

    @pl.loop(0, heads + 3)
    def _(t):
        @pl.when(t < heads)
        def _():
            pl.when(t + AHEAD < heads)(lambda: send_swap((0, 1), t + AHEAD))
            send_swap((2,), t)
            send_direct(t)
            for j in range(1, groups):
                weight_send(t, j, x).start()

        pl.when(jnp.logical_and(t >= 1, t < heads + 1))(lambda: send_relay(t - 1))
        pl.when(jnp.logical_and(t >= 2, t < heads + 2))(lambda: attend_early(t - 2))

        @pl.when(jnp.logical_and(t >= 2, t < heads + 2))
        def _():
            send_on(t - 2)
            for j in range(1, groups):
                weight_send(t - 2, j, source(j)).wait_recv()
                weight_share(t - 2, j, core).start()

        pl.when(jnp.logical_and(t >= 3, t < heads + 3))(lambda: attend_late(t - 3))

    for copy in others:
        copy.wait()

    @pl.loop(0, heads)
    def _(h):
        for j in range(1, groups):
            weight_share(h, j, 1 - core).wait_recv()
            att_send(h, j, source(j)).wait_recv()

    level = levels[0]
    gate_row = gate[pl.ds(level, 1), :]
    width = 2 * HEAD_DIM
    for at in range(0, out.shape[1], width):
        c = slice(at, at + width)
        projected = jnp.dot(att[...], w[:, c], preferred_element_type=jnp.float32)
        out[:, c] = (res[:, c].astype(jnp.float32) + gate_row[:, c] * projected).astype(out.dtype)

    @pl.loop(0, heads)
    def _(h):
        for j in range(1, groups):
            for kind in range(3):
                swap(kind, h, j, x).wait_send()
            weight_send(h, j, x).wait_send()
            weight_share(h, j, core).wait_send()
            att_send(h, j, x).wait_send()
        for kind in range(2):
            for which in (2, 3):
                direct(which, kind, h).wait_send()
            pl.when(has_up)(lambda: direct(0, kind, h).wait_send())
            pl.when(has_down)(lambda: direct(1, kind, h).wait_send())
            pl.when(relays)(lambda: relay(kind, h).wait_send())
            pl.when(passes_on)(lambda: pass_on(kind, h).wait_send())


def body(n, groups, *operands):
    query_rows, gate_table, block_mask, out_weight = (operands[i] for i in (0, 5, 6, 7))
    rows, width = query_rows.shape
    slots, blocks = block_mask.shape[1], block_mask.shape[2]
    frame = rows * groups
    heads = width // HEAD_DIM // groups
    any_space = pl.BlockSpec(memory_space=pltpu.HBM)
    smem = pl.BlockSpec(memory_space=pltpu.SMEM)
    bf16, f32 = jnp.bfloat16, jnp.float32
    dma = pltpu.SemaphoreType.DMA
    pairs = frame * slots * frame * heads
    return pl.pallas_call(
        functools.partial(kernel, n, groups),
        out_shape=jax.ShapeDtypeStruct((rows, width), bf16),
        in_specs=[any_space] * 4 + [smem] + [any_space] * 3,
        out_specs=pl.BlockSpec(memory_space=pltpu.VMEM),
        scratch_shapes=[
            pltpu.VMEM((slots, heads, 2, frame, HEAD_DIM), bf16),
            pltpu.VMEM((heads, frame, HEAD_DIM), bf16),
            pltpu.VMEM((slots - 2, frame, frame), f32),
            pltpu.VMEM((frame, HEAD_DIM), f32),
            pltpu.VMEM((2, frame, HEAD_DIM), f32),
            pltpu.VMEM((2, frame, HEAD_DIM), f32),
            pltpu.VMEM((2, frame, HEAD_DIM), f32),
            pltpu.VMEM((rows, width), bf16),
            pltpu.VMEM((groups - 1, heads, rows, HEAD_DIM), bf16),
            pltpu.VMEM((width, width), bf16),
            pltpu.VMEM((rows, width), bf16),
            pltpu.VMEM(gate_table.shape, f32),
            pltpu.VMEM(block_mask.shape, block_mask.dtype),
            pltpu.VMEM((slots, blocks, frame), f32),
            dma((3, heads)),
            dma((groups - 1, 3, heads)),
            dma((groups - 1, 3, heads)),
            dma((6, 2, heads)),
            dma((slots, 2, heads)),
            dma((groups - 1, heads)),
            dma((groups - 1, heads)),
            dma((groups - 1, heads)),
            dma((groups - 1, heads)),
            dma((groups - 1, heads)),
            dma((groups - 1, heads)),
            dma((4,)),
        ],
        compiler_params=pltpu.CompilerParams(
            collective_id=0, has_side_effects=True, vmem_limit_bytes=60 * 1024 * 1024
        ),
        cost_estimate=pl.CostEstimate(
            flops=4 * pairs * HEAD_DIM + 2 * rows * width * width,
            bytes_accessed=2 * (5 * rows * width + width * width // groups),
            transcendentals=pairs,
        ),
    )(*operands)


def solution(mesh):
    return jax.shard_map(
        functools.partial(body, mesh.shape["ctx"], mesh.shape["head"]),
        mesh=mesh,
        in_specs=(
            P(("ctx", "head"), None),
            P(("ctx", "head"), None),
            P(("ctx", "head"), None),
            P(("ctx", "head"), None),
            P("ctx"),
            P(),
            P("ctx", None, None, None),
            P("head", None),
        ),
        out_specs=P(("ctx", "head"), None),
        check_vma=False,
    )
```

```python
import functools
import math

import jax
import jax.numpy as jnp
from jax import lax
from jax.experimental import pallas as pl
from jax.experimental.pallas import tpu as pltpu
from jax.sharding import PartitionSpec as P

HEAD_DIM = 128
BLOCK = 128
OFFSETS = (0, -1, 1, -2, 2, -4, 4)
MESH = pl.DeviceIdType.MESH
MASKED = -1e30
AHEAD = 2
EXP_SCALE = math.log2(math.e) / math.sqrt(HEAD_DIM)


def kernel(
    n, groups, q_any, k_any, v_any, res_any, levels, gate_any, mask_any, w_any, out,
    kv, qb, s_ref, mx_ref, top_ref, tot_ref, acc_ref, att, att_tx, w, res, gate, mask, bias,
    loc, a2a_tx, a2a_rx, tx, rx, w_tx, w_rx, w_stx, w_srx, att_ts, att_rs, misc,
):
    f = lax.axis_index("ctx")
    x = lax.axis_index("head")
    core = lax.rem(f, 2)
    y = lax.rem(f // 2, 2)
    rows = q_any.shape[0]
    heads = kv.shape[1]
    slots = kv.shape[0]
    frame = kv.shape[3]
    blocks = frame // BLOCK
    depth = w_any.shape[0]
    half = depth // 2
    piece = half // heads
    sib = f + 1 - 2 * core
    pair = f + 2 - 4 * y
    far = f + 4 - 8 * y
    has_up = f + 4 < n
    has_down = f >= 4
    relays = jnp.logical_or(jnp.logical_and(y == 0, has_up), jnp.logical_and(y == 1, has_down))
    passes_on = jnp.logical_or(
        jnp.logical_and(core == 1, f >= 2), jnp.logical_and(core == 0, f + 2 < n)
    )

    def valid(s):
        return jnp.logical_and(f + OFFSETS[s] >= 0, f + OFFSETS[s] < n)

    def peer(j):
        return lax.rem(x + j, groups)

    def source(j):
        return lax.rem(x + groups - j, groups)

    def remote(src, dst, send, recv, dev):
        return pltpu.make_async_remote_copy(
            src_ref=src, dst_ref=dst, send_sem=send, recv_sem=recv,
            device_id=dev, device_id_type=MESH,
        )

    def cols(group, h):
        return pl.ds(pl.multiple_of((group * heads + h) * HEAD_DIM, HEAD_DIM), HEAD_DIM)

    def own_rows(group):
        return pl.ds(pl.multiple_of(group * rows, rows), rows)

    operands = (k_any, v_any, q_any)

    def landing(kind, h, group):
        if kind == 2:
            return qb.at[h, own_rows(group), :]
        return kv.at[0, h, kind, own_rows(group), :]

    def local_in(kind, h):
        return pltpu.make_async_copy(
            operands[kind].at[:, cols(x, h)], landing(kind, h, x), loc.at[kind, h]
        )

    def swap(kind, h, j, group):
        return remote(
            operands[kind].at[:, cols(peer(j), h)], landing(kind, h, group),
            a2a_tx.at[j - 1, kind, h], a2a_rx.at[j - 1, kind, h], (f, peer(j)),
        )

    def direct(which, kind, h):
        slot, dev = ((5, f + 4), (6, f - 4), (3 + y, pair), (1 + core, sib))[which]
        return remote(
            kv.at[0, h, kind], kv.at[slot, h, kind],
            tx.at[which, kind, h], rx.at[slot, kind, h], (dev, x),
        )

    def relay(kind, h):
        if kind == 0:
            src, slot, dev = 4 - y, 3 + y, far
        else:
            src, slot, dev = 6 - y, 4 - y, pair
        return remote(
            kv.at[src, h, kind], kv.at[slot, h, kind],
            tx.at[4, kind, h], rx.at[slot, kind, h], (dev, x),
        )

    def pass_on(kind, h):
        return remote(
            kv.at[4 - core, h, kind], kv.at[2 - core, h, kind],
            tx.at[5, kind, h], rx.at[2 - core, kind, h], (sib, x),
        )

    def wait_slot(slot, kind, h):
        remote(
            kv.at[0, h, kind], kv.at[slot, h, kind],
            tx.at[0, kind, h], rx.at[slot, kind, h], (sib, x),
        ).wait_recv()

    def weight_rows(group, c, t):
        return pl.ds(pl.multiple_of(group * depth + c * half + t * piece, piece), piece)

    def weight_send(t, j, group):
        return remote(
            w_any.at[pl.ds(pl.multiple_of(core * half + t * piece, piece), piece), :],
            w.at[weight_rows(group, core, t), :],
            w_tx.at[j - 1, t], w_rx.at[j - 1, t], (f, peer(j)),
        )

    def weight_share(t, j, c):
        return remote(
            w.at[weight_rows(source(j), core, t), :], w.at[weight_rows(source(j), c, t), :],
            w_stx.at[j - 1, t], w_srx.at[j - 1, t], (sib, x),
        )

    def att_send(h, j, group):
        return remote(
            att_tx.at[j - 1, h], att.at[:, cols(group, h)],
            att_ts.at[j - 1, h], att_rs.at[j - 1, h], (f, peer(j)),
        )

    mask_in = pltpu.make_async_copy(mask_any, mask, misc.at[3])
    mask_in.start()
    others = (
        pltpu.make_async_copy(res_any, res, misc.at[0]),
        pltpu.make_async_copy(gate_any, gate, misc.at[1]),
        pltpu.make_async_copy(
            w_any, w.at[pl.ds(pl.multiple_of(x * depth, depth), depth), :], misc.at[2]
        ),
    )

    barrier = pltpu.get_barrier_semaphore()

    def greet(dev):
        pl.semaphore_signal(barrier, inc=1, device_id=dev, device_id_type=MESH)

    greet((sib, x))
    greet((pair, x))
    for j in range(1, groups):
        greet((f, peer(j)))
    pl.when(has_up)(lambda: greet((f + 4, x)))
    pl.when(has_down)(lambda: greet((f - 4, x)))

    @pl.loop(0, heads)
    def _(h):
        for kind in range(3):
            local_in(kind, h).start()

    pl.semaphore_wait(barrier, 1 + groups + has_up.astype(jnp.int32) + has_down.astype(jnp.int32))

    def send_swap(kinds, h):
        for j in range(1, groups):
            for kind in kinds:
                swap(kind, h, j, x).start()

    for h in range(min(AHEAD, heads)):
        send_swap((0, 1), h)

    for copy in others:
        copy.start()

    mask_in.wait()
    for s in range(slots):
        off = jnp.where(mask[0, s] > 0, 0.0, MASKED)
        for b in range(blocks):
            bias[s, :, b * BLOCK : (b + 1) * BLOCK] = jnp.broadcast_to(
                off[:, b : b + 1], (blocks, BLOCK)
            )

    for s in range(1, slots):

        @pl.when(jnp.logical_not(valid(s)))
        def _():
            @pl.loop(0, heads)
            def _(h):
                for kind in range(2):
                    kv[s, h, kind] = jnp.zeros((frame, HEAD_DIM), kv.dtype)

    def send_direct(h):
        for kind in range(2):
            local_in(kind, h).wait()
            for j in range(1, groups):
                swap(kind, h, j, source(j)).wait_recv()

        @pl.when(has_up)
        def _():
            for kind in range(2):
                direct(0, kind, h).start()

        @pl.when(has_down)
        def _():
            for kind in range(2):
                direct(1, kind, h).start()

        for which in (2, 3):
            for kind in range(2):
                direct(which, kind, h).start()

    def send_relay(h):
        @pl.when(relays)
        def _():
            wait_slot(4 - y, 0, h)
            relay(0, h).start()
            wait_slot(6 - y, 1, h)
            relay(1, h).start()

    def send_on(h):
        @pl.when(passes_on)
        def _():
            for kind in range(2):
                pl.when(core != y)(functools.partial(wait_slot, 4 - core, kind, h))
                pass_on(kind, h).start()

    def early(i):
        picks = (0, 5, 6, 4 - y, 2 - core)
        slot = picks[-1]
        for k in range(len(picks) - 1):
            slot = jnp.where(i == k, picks[k], slot)
        return slot

    def late(i):
        return jnp.where(i == 0, 3 + y, 1 + core)

    def wait_slots(h, now):
        for s in range(1, slots):
            is_late = jnp.logical_or(3 + y == s, 1 + core == s)
            mine = is_late if now == "late" else jnp.logical_not(is_late)
            for kind in range(2):
                known = jnp.logical_and(relays, (4 - y if kind == 0 else 6 - y) == s)
                passed = jnp.logical_and(jnp.logical_and(passes_on, core != y), 3 + y == s)
                due = jnp.logical_and(valid(s), jnp.logical_not(jnp.logical_or(known, passed)))
                pl.when(jnp.logical_and(due, mine))(functools.partial(wait_slot, s, kind, h))

    def fold(h, count, pick, first):
        state = lax.rem(h, 2)
        if first:
            mx_ref[...] = jnp.full_like(mx_ref, MASKED)
        else:
            mx_ref[...] = top_ref[state]

        @pl.loop(0, count, unroll=True)
        def _(i):
            s = pick(i)
            for a in range(blocks):
                r = slice(a * BLOCK, (a + 1) * BLOCK)
                scores = lax.dot_general(
                    qb[h, r], kv[s, h, 0], (((1,), (1,)), ((), ())),
                    preferred_element_type=jnp.float32,
                ) + bias[s, a : a + 1, :]
                s_ref[i, r, :] = scores
                top = mx_ref[r]
                for b in range(blocks):
                    top = jnp.maximum(top, scores[:, b * BLOCK : (b + 1) * BLOCK])
                mx_ref[r] = top

        new_top = jnp.broadcast_to(jnp.max(mx_ref[...], axis=1, keepdims=True), mx_ref.shape)
        if first:
            tot_ref[state] = jnp.zeros(mx_ref.shape, jnp.float32)
            acc_ref[state] = jnp.zeros(mx_ref.shape, jnp.float32)
        else:
            fade = jnp.exp2((top_ref[state] - new_top) * EXP_SCALE)
            tot_ref[state] = tot_ref[state] * fade
            acc_ref[state] = acc_ref[state] * fade
        top_ref[state] = new_top

        @pl.loop(0, count, unroll=True)
        def _(i):
            s = pick(i)
            for a in range(blocks):
                r = slice(a * BLOCK, (a + 1) * BLOCK)
                top = top_ref[state, r]
                total = tot_ref[state, r]
                parts = []
                for b in range(blocks):
                    e = jnp.exp2((s_ref[i, r, b * BLOCK : (b + 1) * BLOCK] - top) * EXP_SCALE)
                    total = total + e
                    parts.append(e.astype(jnp.bfloat16))
                tot_ref[state, r] = total
                acc_ref[state, r] += jnp.dot(
                    jnp.concatenate(parts, axis=1), kv[s, h, 1],
                    preferred_element_type=jnp.float32,
                )

    def attend_early(h):
        local_in(2, h).wait()
        for j in range(1, groups):
            swap(2, h, j, source(j)).wait_recv()
        wait_slots(h, "early")
        fold(h, slots - 2, early, True)

    def attend_late(h):
        wait_slots(h, "late")
        fold(h, 2, late, False)
        state = lax.rem(h, 2)

        def share(group):
            r = own_rows(group)
            total = jnp.sum(tot_ref[state, r, :], axis=1, keepdims=True)
            return (acc_ref[state, r, :] / total).astype(jnp.bfloat16)

        for j in range(1, groups):
            att_tx[j - 1, h] = share(peer(j))
            att_send(h, j, x).start()
        att[:, cols(x, h)] = share(x)

    @pl.loop(0, heads + 3)
    def _(t):
        @pl.when(t < heads)
        def _():
            pl.when(t + AHEAD < heads)(lambda: send_swap((0, 1), t + AHEAD))
            send_swap((2,), t)
            for j in range(1, groups):
                weight_send(t, j, x).start()
            send_direct(t)

        pl.when(jnp.logical_and(t >= 1, t < heads + 1))(lambda: send_relay(t - 1))
        pl.when(jnp.logical_and(t >= 2, t < heads + 2))(lambda: attend_early(t - 2))

        @pl.when(jnp.logical_and(t >= 2, t < heads + 2))
        def _():
            send_on(t - 2)
            for j in range(1, groups):
                weight_send(t - 2, j, source(j)).wait_recv()
                weight_share(t - 2, j, core).start()

        pl.when(jnp.logical_and(t >= 3, t < heads + 3))(lambda: attend_late(t - 3))

    for copy in others:
        copy.wait()

    @pl.loop(0, heads)
    def _(h):
        for j in range(1, groups):
            weight_share(h, j, 1 - core).wait_recv()
            att_send(h, j, source(j)).wait_recv()

    level = levels[0]
    gate_row = gate[pl.ds(level, 1), :]
    width = 2 * HEAD_DIM
    for at in range(0, out.shape[1], width):
        c = slice(at, at + width)
        projected = jnp.dot(att[...], w[:, c], preferred_element_type=jnp.float32)
        out[:, c] = (res[:, c].astype(jnp.float32) + gate_row[:, c] * projected).astype(out.dtype)

    @pl.loop(0, heads)
    def _(h):
        for j in range(1, groups):
            for kind in range(3):
                swap(kind, h, j, x).wait_send()
            weight_send(h, j, x).wait_send()
            weight_share(h, j, core).wait_send()
            att_send(h, j, x).wait_send()
        for kind in range(2):
            for which in (2, 3):
                direct(which, kind, h).wait_send()
            pl.when(has_up)(lambda: direct(0, kind, h).wait_send())
            pl.when(has_down)(lambda: direct(1, kind, h).wait_send())
            pl.when(relays)(lambda: relay(kind, h).wait_send())
            pl.when(passes_on)(lambda: pass_on(kind, h).wait_send())


def body(n, groups, *operands):
    query_rows, gate_table, block_mask, out_weight = (operands[i] for i in (0, 5, 6, 7))
    rows, width = query_rows.shape
    slots, blocks = block_mask.shape[1], block_mask.shape[2]
    frame = rows * groups
    heads = width // HEAD_DIM // groups
    any_space = pl.BlockSpec(memory_space=pltpu.HBM)
    smem = pl.BlockSpec(memory_space=pltpu.SMEM)
    bf16, f32 = jnp.bfloat16, jnp.float32
    dma = pltpu.SemaphoreType.DMA
    pairs = frame * slots * frame * heads
    return pl.pallas_call(
        functools.partial(kernel, n, groups),
        out_shape=jax.ShapeDtypeStruct((rows, width), bf16),
        in_specs=[any_space] * 4 + [smem] + [any_space] * 3,
        out_specs=pl.BlockSpec(memory_space=pltpu.VMEM),
        scratch_shapes=[
            pltpu.VMEM((slots, heads, 2, frame, HEAD_DIM), bf16),
            pltpu.VMEM((heads, frame, HEAD_DIM), bf16),
            pltpu.VMEM((slots - 2, frame, frame), f32),
            pltpu.VMEM((frame, HEAD_DIM), f32),
            pltpu.VMEM((2, frame, HEAD_DIM), f32),
            pltpu.VMEM((2, frame, HEAD_DIM), f32),
            pltpu.VMEM((2, frame, HEAD_DIM), f32),
            pltpu.VMEM((rows, width), bf16),
            pltpu.VMEM((groups - 1, heads, rows, HEAD_DIM), bf16),
            pltpu.VMEM((width, width), bf16),
            pltpu.VMEM((rows, width), bf16),
            pltpu.VMEM(gate_table.shape, f32),
            pltpu.VMEM(block_mask.shape, block_mask.dtype),
            pltpu.VMEM((slots, blocks, frame), f32),
            dma((3, heads)),
            dma((groups - 1, 3, heads)),
            dma((groups - 1, 3, heads)),
            dma((6, 2, heads)),
            dma((slots, 2, heads)),
            dma((groups - 1, heads)),
            dma((groups - 1, heads)),
            dma((groups - 1, heads)),
            dma((groups - 1, heads)),
            dma((groups - 1, heads)),
            dma((groups - 1, heads)),
            dma((4,)),
        ],
        compiler_params=pltpu.CompilerParams(
            collective_id=0, has_side_effects=True, vmem_limit_bytes=60 * 1024 * 1024
        ),
        cost_estimate=pl.CostEstimate(
            flops=4 * pairs * HEAD_DIM + 2 * rows * width * width,
            bytes_accessed=2 * (5 * rows * width + width * width // groups),
            transcendentals=pairs,
        ),
    )(*operands)


def solution(mesh):
    return jax.shard_map(
        functools.partial(body, mesh.shape["ctx"], mesh.shape["head"]),
        mesh=mesh,
        in_specs=(
            P(("ctx", "head"), None),
            P(("ctx", "head"), None),
            P(("ctx", "head"), None),
            P(("ctx", "head"), None),
            P("ctx"),
            P(),
            P("ctx", None, None, None),
            P("head", None),
        ),
        out_specs=P(("ctx", "head"), None),
        check_vma=False,
    )
```
